256 devices in a mesh: dp: 16 (over z, core), mp: 16 (over y, x).
Axes of the slice: x: 4, y: 4, z: 8, core: 2. Of those that a mesh axis runs over, the one named last changes fastest.
Arguments:
- acts: bfloat16 [2048, 8192], P('dp'), may hold values from -6 to 6
- cotangent: bfloat16 [2048, 8192], P('dp', 'mp'), may hold values from -0.01171875 to 0.01171875
- factors: float32 [16, 96, 2, 256, 256], P('dp', 'mp')
- roots: bfloat16 [16, 96, 2, 256, 256], P('dp', 'mp')
- owner_of: int32 [16, 16, 4], replicated, may hold values from 0 to 15, as said below
- slot_of: int32 [16, 16, 4], replicated, may hold values from 0 to 5, as said below
- refresh_ids: int32 [16, 16], replicated, may hold values from 0 to 63, as said below
Outputs:
- direction: float32 [8192, 8192], P('dp', 'mp')
- factors_next: float32 [16, 96, 2, 256, 256], P('dp', 'mp')
- roots_next: bfloat16 [16, 96, 2, 256, 256], P('dp', 'mp')
The draws below stay inside these ranges and needn't reach their ends.
Inputs may be any that keep to these rules, and one draw needn't show every extreme that they name: Within each d, owner_of[d, m, j] names the owner of block j of device (d, m) and slot_of[d, m, j] its slot there; the blocks of one owner have distinct slots; one owner holds at most 6 blocks of a d, and some owner holds exactly 6; at most 1 of one device's blocks go to one owner, reached. `slot_of`: slots as described with owner_of. `refresh_ids`: distinct local ids m * 4 + j; one owner holds at most 2 of a row's refreshed blocks, and some owner exactly that many.
All inputs are finite; a program needn't handle non-finite values.
Results may differ from the reference program's by a relative error of at most 0.0017.
Values may be sent and summed in bfloat16 or wider, within the bound.
No kernel may reach another device: no remote copies, remote signals or barrier semaphores. Data moves between devices by JAX's collectives and lax.ppermute only.
A program may use at most 128 MiB of HBM per device.

```python
import math
import jax
import jax.numpy as jnp
from jax import lax

DIN = 8192
BLOCK = 256
SLAB = 512
ITERS = 10
BLK_DEV = 4
CAP = 6
NREF = 16
TOKENS = 2048
DOUT = 8192
N_DP = 16
N_MP = 16


def layout_row(key):
    keys = jax.random.split(key, 8)
    total = N_MP * BLK_DEV
    owner_perm = jax.random.permutation(keys[0], N_MP)
    shifts = jax.random.randint(keys[1], (N_MP // 2,), 0, BLK_DEV // 2 + 1).at[0].set(BLK_DEV // 2)
    paired = jnp.stack([shifts, -shifts], axis=1).reshape(N_MP)
    loads = jnp.zeros((N_MP,), jnp.int32).at[owner_perm].set(BLK_DEV + paired)
    extra = jax.random.randint(keys[2], (N_MP // 2,), 0, 2).at[0].set(1)
    refresh_perm = jax.random.permutation(keys[3], N_MP)
    counts = jnp.zeros((N_MP,), jnp.int32).at[refresh_perm].set(1 + jnp.stack([extra, -extra], axis=1).reshape(N_MP))
    sequence = jax.random.permutation(keys[4], N_MP)
    ordered = loads[sequence]
    ends = jnp.cumsum(ordered)
    places = jnp.arange(total, dtype=jnp.int32)
    which = jnp.sum((ends[None, :] <= places[:, None]).astype(jnp.int32), axis=1)
    owners = sequence[which]
    ranks = places - (ends - ordered)[which]
    sources = jax.random.permutation(keys[5], N_MP)[places % N_MP]
    local_perm = jax.vmap(lambda part_key: jax.random.permutation(part_key, BLK_DEV))(jax.random.split(keys[6], N_MP))
    position = local_perm[sources, places // N_MP]
    slot_perm = jax.vmap(lambda part_key: jax.random.permutation(part_key, CAP))(jax.random.split(keys[7], N_MP))
    slots = slot_perm[owners, ranks]
    owner_table = jnp.zeros((N_MP, BLK_DEV), jnp.int32).at[sources, position].set(owners)
    slot_table = jnp.zeros((N_MP, BLK_DEV), jnp.int32).at[sources, position].set(slots)
    marked = ranks < counts[owners]
    block_ids = sources * BLK_DEV + position
    keyed = jnp.where(marked, places, places + total)
    first = jnp.argsort(keyed)[:N_MP]
    return (owner_table, slot_table, block_ids[first].astype(jnp.int32))


def layout(key):
    return jax.vmap(layout_row)(jax.random.split(key, N_DP))


def draw_owner_of(key, part):
    return layout(key)[0]


def draw_slot_of(key, part):
    return layout(key)[1]


def draw_refresh_ids(key, part):
    return layout(key)[2]


def draw_factors(key, part):
    key = jax.random.fold_in(key, 5)
    first, second = jax.random.split(key)
    shape = (N_DP, N_MP * CAP, 2, BLOCK, BLOCK)
    identity = jnp.eye(BLOCK, dtype=jnp.float32)
    bound = 0.9 / BLOCK
    logs = jax.random.uniform(first, shape[:4], jnp.float32, -9.0, 1.4)
    noise = jax.random.uniform(second, shape, jnp.float32, -bound, bound)
    diagonal = BLOCK * jnp.exp(logs)
    root_diag = jnp.sqrt(diagonal)
    sym = 0.5 * (noise + jnp.swapaxes(noise, -1, -2)) * (1.0 - identity)
    coupled = root_diag[..., :, None] * sym * root_diag[..., None, :]
    return coupled + diagonal[..., :, None] * identity


def draw_roots(key, part):
    key = jax.random.fold_in(key, 11)
    first, second = jax.random.split(key)
    shape = (N_DP, N_MP * CAP, 2, BLOCK, BLOCK)
    identity = jnp.eye(BLOCK, dtype=jnp.float32)
    diagonal = 0.25 * jnp.exp(jax.random.uniform(first, shape[:4], jnp.float32, -0.7, 0.7))
    noise = jax.random.normal(second, shape, jnp.float32) * (0.25 / math.sqrt(BLOCK))
    return (noise + diagonal[..., :, None] * identity).astype(jnp.bfloat16)


def spiked(entries, stream_key, source, target, blocks, factor):
    owner, partner = [(jnp.arange(entries.shape[dim]) // (entries.shape[dim] // blocks)).reshape([-1 if axis == dim else 1 for axis in range(entries.ndim)]) for dim in (source, target)]
    chosen = jax.random.permutation(stream_key, blocks)[partner]
    strong = (owner == chosen) | (owner == (partner + blocks // 2) % blocks)
    return jnp.where(strong, factor * entries, entries)


def block_levels(own_key, shape, cuts, low, largest):
    factor_of, own = 1.0, jax.random.fold_in(own_key, 6)
    for dim, blocks in cuts:
        draws = jnp.exp(jax.random.uniform(jax.random.fold_in(own, dim), (blocks,), jnp.float32, low / len(cuts), largest / len(cuts)))
        factor_of = factor_of * jnp.repeat(draws, shape[dim] // blocks).reshape([-1 if axis == dim else 1 for axis in range(len(shape))])
    return factor_of


def normal_values(rng, shape, scale, most, pieces=(), kind=jnp.bfloat16):
    values = scale * jax.random.normal(rng, shape, jnp.float32)
    if pieces:
        values = values * block_levels(rng, shape, pieces, -0.22, 0.18)
    return jnp.clip(values, -most, most).astype(kind)


def bell_draw_with(rng, dims, scale, most, cuts, heavy, kind=jnp.bfloat16):
    array = scale * jax.random.normal(rng, dims, jnp.float32)
    if cuts:
        array = array * block_levels(rng, dims, cuts, -0.22, 0.18)
    return jnp.clip(spiked(array, jax.random.fold_in(rng, 3), *heavy), -most, most).astype(kind)


def setup_inputs(seed: int = 0) -> dict:
    arg_keys = jax.random.split(jax.random.key(seed), 8)
    return {
        "acts": bell_draw_with(arg_keys[0], (TOKENS, DIN), 1.0, 6.0, ((0, 16),), (0, 1, 16, 2.0)),
        "cotangent": normal_values(arg_keys[1], (TOKENS, DOUT), (TOKENS * 128) ** -0.5, 0.01171875, ((0, 16), (1, 16))),
        "factors": draw_factors(jax.random.fold_in(arg_keys[7], 71), 0),
        "roots": draw_roots(jax.random.fold_in(arg_keys[7], 71), 0),
        "owner_of": draw_owner_of(jax.random.fold_in(arg_keys[7], 71), 0),
        "slot_of": draw_slot_of(jax.random.fold_in(arg_keys[7], 71), 0),
        "refresh_ids": draw_refresh_ids(jax.random.fold_in(arg_keys[7], 71), 0),
    }


EPSILON = 0.1

def product(left, right):
    return jnp.matmul(left, right, precision=lax.Precision.HIGHEST)

def inverse_root(matrices):
    edge = matrices.shape[-1]
    identity = jnp.eye(edge, dtype=matrices.dtype)
    shifted = matrices + EPSILON * identity
    frob_norm = jnp.sqrt(lax.optimization_barrier(jnp.sum(shifted * shifted, axis=(1, 2), keepdims=True)))
    scaled = shifted / frob_norm
    result = jnp.broadcast_to(identity, matrices.shape) / jnp.sqrt(jnp.sqrt(frob_norm))

    def newton_step(iteration, carry):
        current, moving = carry
        factor = (5.0 * identity - moving) * 0.25
        square = product(factor, factor)
        return (product(current, factor), product(product(square, square), moving))
    result, scaled = lax.fori_loop(0, ITERS, newton_step, (result, scaled))
    return result

def reference(acts, cotangent, factors, roots, owner_of, slot_of, refresh_ids):
    row_blocks = DIN // (N_DP * BLOCK)
    col_blocks = SLAB // BLOCK
    gradient = lax.dot_general(acts, cotangent, (((0,), (0,)), ((), ())), preferred_element_type=jnp.float32)
    blocks = gradient.reshape(N_DP, row_blocks, BLOCK, N_MP, col_blocks, BLOCK)
    blocks = blocks.transpose(0, 3, 1, 4, 2, 5).reshape(N_DP, N_MP * BLK_DEV, BLOCK, BLOCK)
    places = (owner_of * CAP + slot_of).reshape(N_DP, N_MP * BLK_DEV).astype(jnp.int32)
    row_index = jnp.arange(N_DP, dtype=jnp.int32)[:, None]
    previous = factors[row_index, places]
    left_new = previous[:, :, 0] + jnp.einsum('abik,abjk->abij', blocks, blocks, precision=lax.Precision.HIGHEST)
    right_new = previous[:, :, 1] + jnp.einsum('abki,abkj->abij', blocks, blocks, precision=lax.Precision.HIGHEST)
    updated = jnp.stack([left_new, right_new], axis=2)
    factors_next = factors.at[row_index, places].set(updated)
    chosen = updated[row_index, refresh_ids]
    fresh = inverse_root(chosen.reshape(-1, BLOCK, BLOCK)).astype(jnp.bfloat16)
    fresh = fresh.reshape(N_DP, NREF, 2, BLOCK, BLOCK)
    fresh_places = places[row_index, refresh_ids]
    roots_next = roots.at[row_index, fresh_places].set(fresh)
    current = roots_next[row_index, places].astype(jnp.float32)
    precond = product(product(current[:, :, 0], blocks), current[:, :, 1])
    ratio = jnp.sqrt(lax.optimization_barrier(jnp.sum(blocks * blocks, axis=(2, 3))) / (lax.optimization_barrier(jnp.sum(precond * precond, axis=(2, 3))) + 1e-06))
    grafted = precond * ratio[:, :, None, None]
    direction = grafted.reshape(N_DP, N_MP, row_blocks, col_blocks, BLOCK, BLOCK)
    direction = direction.transpose(0, 2, 4, 1, 3, 5).reshape(DIN, N_MP * SLAB)
    return (direction, factors_next, roots_next)
```

```python
import functools

import jax
import jax.numpy as jnp
from jax import lax
from jax.experimental import pallas as pl
from jax.experimental.pallas import tpu as pltpu
from jax.sharding import PartitionSpec as P

ITERS = 10
REFRESH_MOST = 2
EPSILON = 0.1
PAD = 16
TOP_BITS = 14
F32 = jnp.float32
BF16 = jnp.bfloat16
VMEM = pltpu.VMEM
SMEM = pltpu.SMEM


def matmul(left, right, dims=((1,), (0,))):
    return lax.dot_general(left, right, (dims, ((), ())), preferred_element_type=F32)


def split(x):
    high = x.astype(BF16)
    return high, (x - high.astype(F32)).astype(BF16)


def product(left, right):
    lh, ll = left
    rh, rl = right
    return matmul(
        jnp.concatenate([lh, lh, ll], axis=1), jnp.concatenate([rh, rl, rh], axis=0)
    )


def code(block, out_ref, place):
    edge = block.shape[0]
    most = jnp.maximum(jnp.max(jnp.abs(block), axis=(0, 1), keepdims=True), 1e-30)
    shift = TOP_BITS - jnp.floor(jnp.log2(most))
    scaled = jnp.clip(jnp.round(block * jnp.exp2(shift)), -32767.0, 32767.0)
    out_ref[place, :edge, :] = scaled.astype(jnp.int32).astype(jnp.int16)
    out_ref[place, edge:, :] = jnp.broadcast_to(
        shift.astype(jnp.int32), (PAD, block.shape[1])
    ).astype(jnp.int16)


def decode(in_ref, place, edge):
    whole = in_ref[place, :edge, :].astype(jnp.int32).astype(F32)
    shift = in_ref[place, edge:, :].astype(jnp.int32).astype(F32)[:1, :]
    return whole, jnp.exp2(-shift)


def pick_kernel(meta_ref, acts_ref, out_ref):
    parts, rows, tokens = out_ref.shape
    width = acts_ref.shape[1] // parts
    lanes = 128
    mp_index = meta_ref[0]
    group = mp_index * rows // lanes
    inside = lax.rem(mp_index * rows, lanes)
    row = lax.broadcasted_iota(jnp.int32, (rows, lanes), 0)
    col = lax.broadcasted_iota(jnp.int32, (rows, lanes), 1)
    chosen = (col == row + inside).astype(F32).astype(BF16)
    for part in range(parts):
        start = pl.multiple_of(part * width + group * lanes, lanes)
        piece = acts_ref[:, pl.ds(start, lanes)]
        out_ref[part] = matmul(chosen, piece, ((1,), (1,))).astype(BF16)


def gradient_kernel(edge, meta_ref, left_ref, right_ref, out_ref):
    sources, times, rows, tokens = left_ref.shape
    total = sources * rows
    col_blocks = right_ref.shape[1] // edge
    per_edge = edge // rows
    for row_block in range(total // edge):
        pieces = [
            left_ref[row_block * per_edge : (row_block + 1) * per_edge, t].reshape(edge, tokens)
            for t in range(times)
        ]
        strip = jnp.concatenate(pieces, axis=1)
        for col_block in range(col_blocks):
            block = matmul(strip, right_ref[:, col_block * edge : (col_block + 1) * edge])
            code(block, out_ref, meta_ref[2 + row_block * col_blocks + col_block])


def owner_kernel(
    local_blocks,
    meta_ref,
    in_ref,
    factors_hbm,
    roots_hbm,
    factors_out,
    roots_out,
    out_ref,
    state,
    roots,
    moving,
    current,
    table,
    picked,
    state_in,
    state_done,
    roots_sems,
):
    slots, _, edge, _ = state.shape
    sources = in_ref.shape[0]
    ids = sources * local_blocks
    owners, places, fresh = 2 + local_blocks, 2 + local_blocks + ids, 2 + local_blocks + 2 * ids
    refreshed = meta_ref.shape[0] - fresh
    mp_index = meta_ref[0]
    load_roots = pltpu.make_async_copy(roots_hbm, roots, roots_sems.at[0])
    load_roots.start()
    loads = [
        pltpu.make_async_copy(factors_hbm.at[s], state.at[s], state_in.at[s]) for s in range(slots)
    ]
    saves = [
        pltpu.make_async_copy(state.at[s], factors_out.at[s], state_done.at[s])
        for s in range(slots)
    ]
    for load in loads:
        load.start()

    for s in range(slots + 1):
        table[s] = -1
    for s in range(REFRESH_MOST + 1):
        picked[s] = -1

    def place_block(e, carry):
        held = meta_ref[owners + e] == mp_index
        table[jnp.where(held, meta_ref[places + e], slots)] = e // local_blocks
        return carry

    lax.fori_loop(0, ids, place_block, 0)

    def place_fresh(i, count):
        e = meta_ref[fresh + i]
        held = meta_ref[owners + e] == mp_index
        picked[jnp.where(held, count, REFRESH_MOST)] = meta_ref[places + e]
        return count + held.astype(jnp.int32)

    lax.fori_loop(0, refreshed, place_fresh, jnp.int32(0))

    for s in range(slots):
        loads[s].wait()

        @pl.when(table[s] >= 0)
        def _():
            whole, unit = decode(in_ref, table[s], edge)
            high, low = split(whole)
            unit = unit * unit
            left = jnp.concatenate([high, high, low], axis=1)
            right = jnp.concatenate([high, low, high], axis=1)
            state[s, 0] = state[s, 0] + matmul(left, right, ((1,), (1,))) * unit
            left = jnp.concatenate([high, high, low], axis=0)
            right = jnp.concatenate([high, low, high], axis=0)
            state[s, 1] = state[s, 1] + matmul(left, right, ((0,), (0,))) * unit

        saves[s].start()

    row = lax.broadcasted_iota(jnp.int32, (edge, edge), 0)
    col = lax.broadcasted_iota(jnp.int32, (edge, edge), 1)
    identity = (row == col).astype(F32)
    count = REFRESH_MOST * 2
    for b in range(count):
        slot = jnp.maximum(picked[b // 2], 0)
        shifted = state[slot, b % 2] + EPSILON * identity
        norm = jnp.sqrt(jnp.sum(shifted * shifted, axis=(0, 1), keepdims=True))
        scaled = shifted / norm
        factor = (5.0 * identity - scaled) * 0.25
        current[b] = factor / jnp.sqrt(jnp.sqrt(norm))
        half = split(factor)
        half = split(product(half, half))
        half = split(product(half, half))
        moving[b] = product(half, split(scaled))

    def step(iteration, carry):
        old = [moving[b] for b in range(count)]
        factors = [split((5.0 * identity - old[b]) * 0.25) for b in range(count)]
        squares = [split(product(factors[b], factors[b])) for b in range(count)]
        for b in range(count):
            current[b] = product(split(current[b]), factors[b])
        fourth = [split(product(squares[b], squares[b])) for b in range(count)]
        for b in range(count):
            moving[b] = product(fourth[b], split(old[b]))
        return carry

    lax.fori_loop(1, ITERS - 1, step, 0)
    load_roots.wait()
    for b in range(count):
        factor = split((5.0 * identity - moving[b]) * 0.25)
        final = product(split(current[b]), factor).astype(BF16)

        @pl.when(picked[b // 2] >= 0)
        def _():
            roots[picked[b // 2], b % 2] = final

    save_roots = pltpu.make_async_copy(roots, roots_out, roots_sems.at[1])
    save_roots.start()

    for s in range(slots):

        @pl.when(table[s] >= 0)
        def _():
            whole, unit = decode(in_ref, table[s], edge)
            high, low = split(whole)
            left = roots[s, 0]
            right = roots[s, 1]
            first = matmul(
                jnp.concatenate([left, left], axis=1), jnp.concatenate([high, low], axis=0)
            )
            fh, fl = split(first)
            precond = matmul(
                jnp.concatenate([fh, fl], axis=1), jnp.concatenate([right, right], axis=0)
            )
            precond = precond * unit
            block = whole * unit
            block_sum = jnp.sum(block * block, axis=(0, 1), keepdims=True)
            precond_sum = jnp.sum(precond * precond, axis=(0, 1), keepdims=True)
            ratio = jnp.sqrt(block_sum / (precond_sum + 1e-06))
            code(precond * ratio, out_ref, table[s])

    save_roots.wait()
    for save in saves:
        save.wait()


def home_kernel(edge, meta_ref, in_ref, out_ref):
    col_blocks = out_ref.shape[1] // edge
    for j in range((out_ref.shape[0] // edge) * col_blocks):
        top, left = (j // col_blocks) * edge, (j % col_blocks) * edge
        whole, unit = decode(in_ref, meta_ref[2 + j], edge)
        out_ref[top : top + edge, left : left + edge] = whole * unit


def body(acts, cotangent, factors, roots, owner_of, slot_of, refresh_ids):
    dp_count = lax.axis_size("dp")
    mp_count = lax.axis_size("mp")
    dp_index = lax.axis_index("dp")
    mp_index = lax.axis_index("mp")
    edge = factors.shape[-1]
    slots = factors.shape[1]
    tokens = acts.shape[0]
    row_count = acts.shape[1] // dp_count
    slab = cotangent.shape[1]
    local_blocks = owner_of.shape[2]
    rows = row_count // mp_count

    gathered = lax.all_gather(cotangent, "dp", axis=0, tiled=True)

    owners = lax.dynamic_index_in_dim(owner_of, dp_index, 0, keepdims=False)
    places = lax.dynamic_index_in_dim(slot_of, dp_index, 0, keepdims=False)
    fresh = lax.dynamic_index_in_dim(refresh_ids, dp_index, 0, keepdims=False)
    mine = lax.dynamic_index_in_dim(owners, mp_index, 0, keepdims=False)
    meta = jnp.concatenate(
        [
            jnp.stack([mp_index, dp_index]).astype(jnp.int32),
            mine,
            owners.reshape(-1),
            places.reshape(-1),
            fresh,
        ]
    )

    smem = pl.BlockSpec(memory_space=SMEM)
    vmem = pl.BlockSpec(memory_space=VMEM)
    hbm = pl.BlockSpec(memory_space=pl.ANY)

    picked = pl.pallas_call(
        pick_kernel,
        out_shape=jax.ShapeDtypeStruct((dp_count, rows, tokens), BF16),
        in_specs=[smem, vmem],
        out_specs=vmem,
    )(mp_index.astype(jnp.int32).reshape(1), acts)
    picked = lax.all_to_all(picked, "dp", split_axis=0, concat_axis=0, tiled=True)
    spread = jnp.broadcast_to(picked[None], (mp_count, dp_count, rows, tokens))
    left = lax.all_to_all(spread, "mp", split_axis=0, concat_axis=0, tiled=True)

    coded = jax.ShapeDtypeStruct((mp_count, edge + PAD, edge), jnp.int16)
    outgoing = pl.pallas_call(
        functools.partial(gradient_kernel, edge),
        out_shape=coded,
        in_specs=[smem, vmem, vmem],
        out_specs=vmem,
        compiler_params=pltpu.CompilerParams(vmem_limit_bytes=32 * 1024 * 1024),
    )(meta, left, gathered)
    incoming = lax.all_to_all(outgoing, "mp", split_axis=0, concat_axis=0, tiled=True)

    count = REFRESH_MOST * 2
    factors_next, roots_next, homeward = pl.pallas_call(
        functools.partial(owner_kernel, local_blocks),
        out_shape=(
            jax.ShapeDtypeStruct(factors.shape[1:], F32),
            jax.ShapeDtypeStruct(roots.shape[1:], BF16),
            coded,
        ),
        in_specs=[smem, vmem, hbm, hbm],
        out_specs=(hbm, hbm, vmem),
        scratch_shapes=[
            VMEM(factors.shape[1:], F32),
            VMEM(roots.shape[1:], BF16),
            VMEM((count, edge, edge), F32),
            VMEM((count, edge, edge), F32),
            SMEM((slots + 1,), jnp.int32),
            SMEM((REFRESH_MOST + 1,), jnp.int32),
            pltpu.SemaphoreType.DMA((slots,)),
            pltpu.SemaphoreType.DMA((slots,)),
            pltpu.SemaphoreType.DMA((2,)),
        ],
        compiler_params=pltpu.CompilerParams(vmem_limit_bytes=40 * 1024 * 1024),
    )(meta, incoming, factors[0], roots[0])
    returned = lax.all_to_all(homeward, "mp", split_axis=0, concat_axis=0, tiled=True)

    direction = pl.pallas_call(
        functools.partial(home_kernel, edge),
        out_shape=jax.ShapeDtypeStruct((row_count, slab), F32),
        in_specs=[smem, vmem],
        out_specs=vmem,
    )(meta, returned)
    return (direction, factors_next[None], roots_next[None])


def solution(mesh):
    in_specs = (
        P("dp", None),
        P("dp", "mp"),
        P("dp", "mp", None, None, None),
        P("dp", "mp", None, None, None),
        P(),
        P(),
        P(),
    )
    out_specs = (P("dp", "mp"), P("dp", "mp", None, None, None), P("dp", "mp", None, None, None))
    return jax.shard_map(body, mesh=mesh, in_specs=in_specs, out_specs=out_specs, check_vma=False)
```

```python
import functools

import jax
import jax.numpy as jnp
from jax import lax
from jax.experimental import pallas as pl
from jax.experimental.pallas import tpu as pltpu
from jax.sharding import PartitionSpec as P

ITERS = 10
REFRESH_MOST = 2
EPSILON = 0.1
PAD = 16
TOP_BITS = 14
F32 = jnp.float32
BF16 = jnp.bfloat16
VMEM = pltpu.VMEM
SMEM = pltpu.SMEM


def matmul(left, right, dims=((1,), (0,))):
    return lax.dot_general(left, right, (dims, ((), ())), preferred_element_type=F32)


def split(x):
    high = x.astype(BF16)
    return high, (x - high.astype(F32)).astype(BF16)


def product(left, right):
    lh, ll = left
    rh, rl = right
    return matmul(
        jnp.concatenate([lh, lh, ll], axis=1), jnp.concatenate([rh, rl, rh], axis=0)
    )


def quantized(values, shift):
    scaled = jnp.clip(jnp.round(values * jnp.exp2(shift)), -32767.0, 32767.0)
    return scaled.astype(jnp.int32).astype(jnp.int16)


def code(block, out_ref, place):
    edge = block.shape[0]
    most = jnp.maximum(jnp.max(jnp.abs(block), axis=(0, 1), keepdims=True), 1e-30)
    shift = TOP_BITS - jnp.floor(jnp.log2(most))
    out_ref[place, :edge, :] = quantized(block, shift)
    out_ref[place, edge:, :] = jnp.broadcast_to(
        shift.astype(jnp.int32), (PAD, block.shape[1])
    ).astype(jnp.int16)


def decode(in_ref, place, edge):
    whole = in_ref[place, :edge, :].astype(jnp.int32).astype(F32)
    shift = in_ref[place, edge:, :].astype(jnp.int32).astype(F32)[:1, :]
    return whole, jnp.exp2(-shift)


def pick_kernel(acts_ref, out_ref):
    parts, rows, tokens = out_ref.shape
    width = acts_ref.shape[1] // parts
    lanes = 128
    mp_index = lax.axis_index("mp")
    group = mp_index * rows // lanes
    inside = lax.rem(mp_index * rows, lanes)
    row = lax.broadcasted_iota(jnp.int32, (rows, lanes), 0)
    col = lax.broadcasted_iota(jnp.int32, (rows, lanes), 1)
    chosen = (col == row + inside).astype(F32).astype(BF16)
    for part in range(parts):
        start = pl.multiple_of(part * width + group * lanes, lanes)
        piece = acts_ref[:, pl.ds(start, lanes)]
        out_ref[part] = matmul(chosen, piece, ((1,), (1,))).astype(BF16)


def strip_kernel(edge, cot_ref, out_ref):
    owners, rows, lanes = out_ref.shape
    blocks = cot_ref.shape[1] // edge
    depth = rows // blocks
    row = lax.broadcasted_iota(jnp.int32, (lanes, lanes), 0)
    col = lax.broadcasted_iota(jnp.int32, (lanes, lanes), 1)
    identity = (row == col).astype(F32).astype(BF16)
    for chunk in range(cot_ref.shape[1] // lanes):
        piece = cot_ref[:, chunk * lanes : (chunk + 1) * lanes]
        turned = matmul(identity, piece, ((1,), (1,))).astype(BF16)
        block, first = divmod(chunk * lanes, edge)
        for k in range(lanes // depth):
            out_ref[first // depth + k, block * depth : (block + 1) * depth, :] = turned[
                k * depth : (k + 1) * depth
            ]


def gradient_kernel(edge, slots, owner_ref, place_ref, left_hbm, *refs):
    rights_hbm, (out_ref, left_ref, rights, shifts, sems) = refs[:-5], refs[-5:]
    sources, times, rows, tokens = left_ref.shape
    copies = [pltpu.make_async_copy(left_hbm, left_ref, sems.at[times])] + [
        pltpu.make_async_copy(rights_hbm[k], rights.at[k], sems.at[k]) for k in range(times)
    ]
    for copy in copies:
        copy.start()
    depth = edge // sources
    dp_index = lax.axis_index("dp")
    shifts[...] = jnp.zeros_like(shifts)
    total = sources * rows
    when = [token_group(dp_index, times, k) for k in range(times)]
    for copy in copies:
        copy.wait()
    left = jnp.concatenate([left_ref[:, t].reshape(total, tokens) for t in when], axis=1)
    slab = rights.shape[1]
    col_blocks = slab // (sources * depth)
    for chunk in range(slab // edge):
        strips = jnp.concatenate(
            [rights[k, chunk * edge : (chunk + 1) * edge, :] for k in range(times)], axis=1
        )
        product_t = matmul(strips, left, ((1,), (1,))).reshape(edge // depth, depth, total)
        for row_block in range(total // edge):
            values = product_t[:, :, row_block * edge : (row_block + 1) * edge]
            most = jnp.max(jnp.abs(values), axis=(1, 2), keepdims=True)
            shift = TOP_BITS - jnp.floor(jnp.log2(jnp.maximum(most, 1e-30)))
            coded = quantized(values, shift)
            for k in range(edge // depth):
                m, col_block = divmod(chunk * (edge // depth) + k, col_blocks)
                j = row_block * col_blocks + col_block
                owner, place = owner_ref[dp_index, j, m], place_ref[dp_index, j, m]
                top = pl.multiple_of(place * depth, depth)
                out_ref[owner, pl.ds(top, depth), :] = coded[k]
                shifts[owner, pl.ds(place, 1), :] = jnp.broadcast_to(shift[k], (1, edge))
    out_ref[:, slots * depth :, :] = shifts[...].astype(jnp.int32).astype(jnp.int16)


def ring_offsets(chips):
    offsets = [0]
    for step in range(1, chips // 2):
        offsets += [-step, step]
    return offsets + [-(chips // 2)]


def token_group(dp_index, times, k):
    chips = times // 2
    offset = ring_offsets(chips)[k % chips]
    core = lax.rem(dp_index, 2)
    core = core if k < chips else 1 - core
    return lax.rem(dp_index // 2 + (offset + chips), chips) * 2 + core


def owner_kernel(
    owner_ref,
    place_ref,
    fresh_ref,
    in_ref,
    factors_hbm,
    roots_hbm,
    factors_out,
    roots_out,
    out_ref,
    state,
    roots,
    units,
    halves,
    moving,
    current,
    table,
    picked,
    state_in,
    state_done,
    roots_sems,
):
    slots, _, edge, _ = state.shape
    local_blocks, sources = owner_ref.shape[1:]
    dp_index, mp_index = lax.axis_index("dp"), lax.axis_index("mp")
    load_roots = pltpu.make_async_copy(roots_hbm, roots, roots_sems.at[0])
    load_roots.start()
    loads = [
        pltpu.make_async_copy(factors_hbm.at[s], state.at[s], state_in.at[s]) for s in range(slots)
    ]
    saves = [
        pltpu.make_async_copy(state.at[s], factors_out.at[s], state_done.at[s])
        for s in range(slots)
    ]
    for load in loads:
        load.start()

    for s in range(slots + 1):
        table[s] = -1
    for s in range(REFRESH_MOST + 1):
        picked[s] = -1

    def place_source(m, carry):
        for j in range(local_blocks):
            held = owner_ref[dp_index, j, m] == mp_index
            table[jnp.where(held, place_ref[dp_index, j, m], slots)] = m
        return carry

    lax.fori_loop(0, sources, place_source, 0)

    def place_fresh(i, count):
        block = fresh_ref[dp_index, i]
        m, j = block // local_blocks, lax.rem(block, local_blocks)
        held = owner_ref[dp_index, j, m] == mp_index
        picked[jnp.where(held, count, REFRESH_MOST)] = place_ref[dp_index, j, m]
        return count + held.astype(jnp.int32)

    lax.fori_loop(0, fresh_ref.shape[1], place_fresh, jnp.int32(0))

    depth = edge // sources
    units[...] = jnp.exp2(-in_ref[:, slots * depth :, :].astype(jnp.int32).astype(F32))
    for s in range(slots):
        loads[s].wait()

        @pl.when(table[s] >= 0)
        def _():
            whole = in_ref[:, s * depth : (s + 1) * depth, :].astype(jnp.int32).astype(F32)
            high, low = split((whole * units[:, s : s + 1, :]).reshape(edge, edge))
            halves[s, 0] = high
            halves[s, 1] = low
            left = jnp.concatenate([high, high, low], axis=0)
            right = jnp.concatenate([high, low, high], axis=0)
            state[s, 0] = state[s, 0] + matmul(left, right, ((0,), (0,)))
            left = jnp.concatenate([high, high, low], axis=1)
            right = jnp.concatenate([high, low, high], axis=1)
            state[s, 1] = state[s, 1] + matmul(left, right, ((1,), (1,)))

        saves[s].start()

    row = lax.broadcasted_iota(jnp.int32, (edge, edge), 0)
    col = lax.broadcasted_iota(jnp.int32, (edge, edge), 1)
    identity = (row == col).astype(F32)
    count = REFRESH_MOST * 2
    for b in range(count):
        slot = jnp.maximum(picked[b // 2], 0)
        shifted = state[slot, b % 2] + EPSILON * identity
        norm = jnp.sqrt(jnp.sum(shifted * shifted, axis=(0, 1), keepdims=True))
        scaled = shifted / norm
        factor = (5.0 * identity - scaled) * 0.25
        current[b] = factor / jnp.sqrt(jnp.sqrt(norm))
        half = split(factor)
        half = split(product(half, half))
        half = split(product(half, half))
        moving[b] = product(half, split(scaled))

    def step(iteration, carry):
        old = [moving[b] for b in range(count)]
        factors = [split((5.0 * identity - old[b]) * 0.25) for b in range(count)]
        squares = [split(product(factors[b], factors[b])) for b in range(count)]
        for b in range(count):
            current[b] = product(split(current[b]), factors[b])
        fourth = [split(product(squares[b], squares[b])) for b in range(count)]
        for b in range(count):
            moving[b] = product(fourth[b], split(old[b]))
        return carry

    lax.fori_loop(1, ITERS - 1, step, 0)
    load_roots.wait()
    for b in range(count):
        factor = split((5.0 * identity - moving[b]) * 0.25)
        final = product(split(current[b]), factor).astype(BF16)

        @pl.when(picked[b // 2] >= 0)
        def _():
            roots[picked[b // 2], b % 2] = final

    save_roots = pltpu.make_async_copy(roots, roots_out, roots_sems.at[1])
    save_roots.start()

    for s in range(slots):

        @pl.when(table[s] >= 0)
        def _():
            high, low = halves[s, 0], halves[s, 1]
            left = roots[s, 0]
            right = roots[s, 1]
            first = matmul(
                jnp.concatenate([high, low], axis=0),
                jnp.concatenate([right, right], axis=0),
                ((0,), (0,)),
            )
            fh, fl = split(first)
            precond = matmul(
                jnp.concatenate([left, left], axis=1), jnp.concatenate([fh, fl], axis=0)
            )
            block = high.astype(F32) + low.astype(F32)
            block_sum = jnp.sum(block * block, axis=(0, 1), keepdims=True)
            precond_sum = jnp.sum(precond * precond, axis=(0, 1), keepdims=True)
            ratio = jnp.sqrt(block_sum / (precond_sum + 1e-06))
            code(precond * ratio, out_ref, table[s])

    save_roots.wait()
    for save in saves:
        save.wait()


def home_kernel(edge, owner_ref, in_hbm, out_ref, blocks, sems):
    dp_index, mp_index = lax.axis_index("dp"), lax.axis_index("mp")
    col_blocks = out_ref.shape[1] // edge
    copies = [
        pltpu.make_async_copy(
            in_hbm.at[owner_ref[dp_index, j, mp_index]], blocks.at[j], sems.at[j]
        )
        for j in range(blocks.shape[0])
    ]
    for copy in copies:
        copy.start()
    for j, copy in enumerate(copies):
        copy.wait()
        top, left = (j // col_blocks) * edge, (j % col_blocks) * edge
        whole, unit = decode(blocks, j, edge)
        out_ref[top : top + edge, left : left + edge] = whole * unit


def body(acts, cotangent, factors, roots, owner_of, slot_of, refresh_ids):
    dp_count = lax.axis_size("dp")
    mp_count = lax.axis_size("mp")
    edge = factors.shape[-1]
    slots = factors.shape[1]
    tokens = acts.shape[0]
    row_count = acts.shape[1] // dp_count
    slab = cotangent.shape[1]
    rows = row_count // mp_count
    owner_of = owner_of.transpose(0, 2, 1)
    slot_of = slot_of.transpose(0, 2, 1)

    smem = pl.BlockSpec(memory_space=SMEM)
    vmem = pl.BlockSpec(memory_space=VMEM)
    hbm = pl.BlockSpec(memory_space=pl.ANY)

    up = [(i, (i + 2) % dp_count) for i in range(dp_count)]
    down = [(i, (i - 2) % dp_count) for i in range(dp_count)]
    swap = [(i, i ^ 1) for i in range(dp_count)]

    picked = pl.pallas_call(
        pick_kernel,
        out_shape=jax.ShapeDtypeStruct((dp_count, rows, tokens), BF16),
        in_specs=[vmem],
        out_specs=vmem,
    )(acts)

    def ring(above, below):
        return lax.ppermute(above, "dp", up), lax.ppermute(below, "dp", down)

    def swapped(x):
        return lax.ppermute(x, "dp", swap)

    strips = pl.pallas_call(
        functools.partial(strip_kernel, edge),
        out_shape=jax.ShapeDtypeStruct((mp_count, slab // mp_count, tokens), BF16),
        in_specs=[vmem],
        out_specs=vmem,
    )(cotangent)
    strips = lax.all_to_all(strips, "mp", split_axis=0, concat_axis=0, tiled=True)
    strips = strips.reshape(slab, tokens)
    first = ring(strips, strips)
    own = lax.all_to_all(picked, "dp", split_axis=0, concat_axis=0, tiled=True)
    own, first = lax.optimization_barrier((own, first))
    spread = jnp.broadcast_to(own[None], (mp_count, dp_count, rows, tokens))
    left = lax.all_to_all(spread, "mp", split_axis=0, concat_axis=0, tiled=True)
    second = ring(*first)
    third = ring(*second)
    third_swapped = [swapped(x) for x in third]
    last = ring(third[0], third_swapped[1])
    same = [strips, *first, *second, *third, last[0]]
    gathered = same + [swapped(x) for x in same[:5]] + third_swapped + [last[1]]

    depth = edge // mp_count
    outgoing = pl.pallas_call(
        functools.partial(gradient_kernel, edge, slots),
        out_shape=jax.ShapeDtypeStruct((mp_count, slots * depth + PAD, edge), jnp.int16),
        in_specs=[smem, smem, hbm] + [hbm] * len(gathered),
        out_specs=vmem,
        scratch_shapes=[
            VMEM((mp_count, dp_count, rows, tokens), BF16),
            VMEM((dp_count, slab, tokens), BF16),
            VMEM((mp_count, PAD, edge), F32),
            pltpu.SemaphoreType.DMA((dp_count + 1,)),
        ],
        compiler_params=pltpu.CompilerParams(vmem_limit_bytes=60 * 1024 * 1024),
    )(owner_of, slot_of, left, *gathered)
    incoming = lax.all_to_all(outgoing, "mp", split_axis=0, concat_axis=0, tiled=True)

    count = REFRESH_MOST * 2
    factors_next, roots_next, homeward = pl.pallas_call(
        owner_kernel,
        out_shape=(
            jax.ShapeDtypeStruct(factors.shape[1:], F32),
            jax.ShapeDtypeStruct(roots.shape[1:], BF16),
            jax.ShapeDtypeStruct((mp_count, edge + PAD, edge), jnp.int16),
        ),
        in_specs=[smem, smem, smem, vmem, hbm, hbm],
        out_specs=(hbm, hbm, vmem),
        scratch_shapes=[
            VMEM(factors.shape[1:], F32),
            VMEM(roots.shape[1:], BF16),
            VMEM((mp_count, PAD, edge), F32),
            VMEM((slots, 2, edge, edge), BF16),
            VMEM((count, edge, edge), F32),
            VMEM((count, edge, edge), F32),
            SMEM((slots + 1,), jnp.int32),
            SMEM((REFRESH_MOST + 1,), jnp.int32),
            pltpu.SemaphoreType.DMA((slots,)),
            pltpu.SemaphoreType.DMA((slots,)),
            pltpu.SemaphoreType.DMA((2,)),
        ],
        compiler_params=pltpu.CompilerParams(vmem_limit_bytes=28 * 1024 * 1024),
    )(owner_of, slot_of, refresh_ids, incoming, factors[0], roots[0])
    returned = lax.all_to_all(homeward, "mp", split_axis=0, concat_axis=0, tiled=True)

    local_blocks = owner_of.shape[1]
    direction = pl.pallas_call(
        functools.partial(home_kernel, edge),
        out_shape=jax.ShapeDtypeStruct((row_count, slab), F32),
        in_specs=[smem, hbm],
        out_specs=vmem,
        scratch_shapes=[
            VMEM((local_blocks, edge + PAD, edge), jnp.int16),
            pltpu.SemaphoreType.DMA((local_blocks,)),
        ],
    )(owner_of, returned)
    return (direction, factors_next[None], roots_next[None])


def solution(mesh):
    in_specs = (
        P("dp", None),
        P("dp", "mp"),
        P("dp", "mp", None, None, None),
        P("dp", "mp", None, None, None),
        P(),
        P(),
        P(),
    )
    out_specs = (P("dp", "mp"), P("dp", "mp", None, None, None), P("dp", "mp", None, None, None))
    return jax.shard_map(body, mesh=mesh, in_specs=in_specs, out_specs=out_specs, check_vma=False)
```

```python
import functools
import math

import jax
import jax.numpy as jnp
from jax import lax
from jax.experimental import pallas as pl
from jax.experimental.pallas import tpu as pltpu
from jax.sharding import PartitionSpec as P

ITERS = 10
REFRESH_MOST = 2
EPSILON = 0.1
PAD = 16
TOP_BITS = 14
MIDDLE = 1.125
F32 = jnp.float32
BF16 = jnp.bfloat16
VMEM = pltpu.VMEM
SMEM = pltpu.SMEM


def matmul(left, right, dims=((1,), (0,))):
    return lax.dot_general(left, right, (dims, ((), ())), preferred_element_type=F32)


def split(x):
    high = x.astype(BF16)
    return high, (x - high.astype(F32)).astype(BF16)


def product(left, right):
    lh, ll = left
    rh, rl = right
    return matmul(
        jnp.concatenate([lh, lh, ll], axis=1), jnp.concatenate([rh, rl, rh], axis=0)
    )


def quantized(values, shift):
    scaled = jnp.clip(jnp.round(values * jnp.exp2(shift)), -32767.0, 32767.0)
    return scaled.astype(jnp.int32).astype(jnp.int16)


def code(block, out_ref, place):
    edge = block.shape[0]
    most = jnp.maximum(jnp.max(jnp.abs(block), axis=(0, 1), keepdims=True), 1e-30)
    shift = TOP_BITS - jnp.floor(jnp.log2(most))
    out_ref[place, :edge, :] = quantized(block, shift)
    out_ref[place, edge:, :] = jnp.broadcast_to(
        shift.astype(jnp.int32), (PAD, block.shape[1])
    ).astype(jnp.int16)


def decode(in_ref, place, edge):
    whole = in_ref[place, :edge, :].astype(jnp.int32).astype(F32)
    shift = in_ref[place, edge:, :].astype(jnp.int32).astype(F32)[:1, :]
    return whole, jnp.exp2(-shift)


def position(ways):
    mp_index = lax.axis_index("mp")
    return mp_index // ways, lax.rem(mp_index, ways)


def pick_kernel(edge, acts_ref, out_ref):
    parts, rows, tokens = out_ref.shape
    half = rows // 2
    width = acts_ref.shape[1] // parts
    lanes = 128
    row = lax.broadcasted_iota(jnp.int32, (half, lanes), 0)
    col = lax.broadcasted_iota(jnp.int32, (half, lanes), 1)
    for side in range(2):
        first = position(edge // half)[side] * half
        group = first // lanes
        inside = lax.rem(first, lanes)
        chosen = (col == row + inside).astype(F32).astype(BF16)
        for part in range(parts):
            start = pl.multiple_of(part * width + side * edge + group * lanes, lanes)
            piece = acts_ref[:, pl.ds(start, lanes)]
            out_ref[part, side * half : (side + 1) * half, :] = matmul(
                chosen, piece, ((1,), (1,))
            ).astype(BF16)


def strip_kernel(edge, cot_ref, out_ref):
    owners, rows, lanes = out_ref.shape
    blocks = cot_ref.shape[1] // edge
    depth = rows // blocks
    row = lax.broadcasted_iota(jnp.int32, (lanes, lanes), 0)
    col = lax.broadcasted_iota(jnp.int32, (lanes, lanes), 1)
    identity = (row == col).astype(F32).astype(BF16)
    for chunk in range(cot_ref.shape[1] // lanes):
        piece = cot_ref[:, chunk * lanes : (chunk + 1) * lanes]
        turned = matmul(identity, piece, ((1,), (1,))).astype(BF16)
        block, first = divmod(chunk * lanes, edge)
        for k in range(lanes // depth):
            out_ref[first // depth + k, block * depth : (block + 1) * depth, :] = turned[
                k * depth : (k + 1) * depth
            ]


def gradient_kernel(edge, slots, owner_ref, place_ref, own_hbm, *refs):
    out_ref, left, rights, shifts, sems = refs[-5:]
    chips = rights.shape[0]
    rights_hbm, lefts_hbm = refs[-5 - chips : -5], refs[: -5 - chips]
    times, rows, tokens = own_hbm.shape
    half = rows // 2
    ways = edge // half
    sources = ways * ways
    depth = edge // sources
    dp_index = lax.axis_index("dp")
    copies = [(rights_hbm[k], rights.at[k]) for k in range(chips)]
    for side, place in enumerate(position(ways)):
        for away in range(ways):
            part = lax.rem(place + (ways - away), ways)
            top = pl.multiple_of(side * edge + part * half, half)
            if away == 0:
                source = own_hbm.at[:, side * half : (side + 1) * half, :]
            else:
                source = lefts_hbm[side * (ways - 1) + away - 1]
            copies.append((source, left.at[:, pl.ds(top, half), :]))
    copies = [
        pltpu.make_async_copy(source, target, sems.at[i])
        for i, (source, target) in enumerate(copies)
    ]
    for copy in copies:
        copy.start()
    shifts[...] = jnp.zeros_like(shifts)
    total = left.shape[1]
    when = token_groups(dp_index, chips)
    for copy in copies:
        copy.wait()
    left = jnp.concatenate([left[t] for t in when], axis=1)
    slab = rights.shape[2]
    col_blocks = slab // (sources * depth)
    for chunk in range(slab // edge):
        strips = jnp.concatenate(
            [rights[k // 2, k % 2, chunk * edge : (chunk + 1) * edge, :] for k in range(times)],
            axis=1,
        )
        product_t = matmul(strips, left, ((1,), (1,))).reshape(edge // depth, depth, total)
        for row_block in range(total // edge):
            values = product_t[:, :, row_block * edge : (row_block + 1) * edge]
            most = jnp.max(jnp.abs(values), axis=(1, 2), keepdims=True)
            shift = TOP_BITS - jnp.floor(jnp.log2(jnp.maximum(most, 1e-30)))
            coded = quantized(values, shift)
            for k in range(edge // depth):
                m, col_block = divmod(chunk * (edge // depth) + k, col_blocks)
                j = row_block * col_blocks + col_block
                owner, place = owner_ref[dp_index, j, m], place_ref[dp_index, j, m]
                top = pl.multiple_of(place * depth, depth)
                out_ref[owner, pl.ds(top, depth), :] = coded[k]
                shifts[owner, pl.ds(place, 1), :] = jnp.broadcast_to(shift[k], (1, edge))
    out_ref[:, slots * depth :, :] = shifts[...].astype(jnp.int32).astype(jnp.int16)


def token_groups(dp_index, chips):
    chip, core = dp_index // 2, lax.rem(dp_index, 2)
    away = 1 - 2 * core
    groups = [2 * chip + core, 2 * chip + 1 - core]
    for step in range(1, chips // 2 + 1):
        for side in (-1, 1)[: 2 if step < chips // 2 else 1]:
            first = core if side < 0 else 1 - core
            base = 2 * lax.rem(chip + side * step * away + chips, chips)
            groups += [base + first, base + 1 - first]
    return groups


def owner_kernel(
    owner_ref,
    place_ref,
    fresh_ref,
    in_ref,
    factors_hbm,
    roots_hbm,
    factors_out,
    roots_out,
    out_ref,
    state,
    roots,
    units,
    halves,
    results,
    moving,
    current,
    table,
    picked,
    state_in,
    state_done,
    roots_sems,
):
    slots, _, edge, _ = state.shape
    local_blocks, sources = owner_ref.shape[1:]
    dp_index, mp_index = lax.axis_index("dp"), lax.axis_index("mp")
    load_roots = pltpu.make_async_copy(roots_hbm, roots, roots_sems.at[0])
    load_roots.start()
    loads = [
        pltpu.make_async_copy(factors_hbm.at[s], state.at[s], state_in.at[s]) for s in range(slots)
    ]
    saves = [
        pltpu.make_async_copy(state.at[s], factors_out.at[s], state_done.at[s])
        for s in range(slots)
    ]
    for load in loads:
        load.start()

    for s in range(slots + 1):
        table[s] = -1
    for s in range(REFRESH_MOST + 1):
        picked[s] = -1

    def place_source(m, carry):
        for j in range(local_blocks):
            held = owner_ref[dp_index, j, m] == mp_index
            table[jnp.where(held, place_ref[dp_index, j, m], slots)] = m
        return carry

    lax.fori_loop(0, sources, place_source, 0)

    def place_fresh(i, count):
        block = fresh_ref[dp_index, i]
        m, j = block // local_blocks, lax.rem(block, local_blocks)
        held = owner_ref[dp_index, j, m] == mp_index
        picked[jnp.where(held, count, REFRESH_MOST)] = place_ref[dp_index, j, m]
        return count + held.astype(jnp.int32)

    lax.fori_loop(0, fresh_ref.shape[1], place_fresh, jnp.int32(0))

    depth = edge // sources
    units[...] = jnp.exp2(-in_ref[:, slots * depth :, :].astype(jnp.int32).astype(F32))
    for load in loads:
        load.wait()
    for s in range(slots):
        whole = in_ref[:, s * depth : (s + 1) * depth, :].astype(jnp.int32).astype(F32)
        block = jnp.where(table[s] >= 0, whole * units[:, s : s + 1, :], 0.0)
        high, low = split(block.reshape(edge, edge))
        halves[s, 0] = high
        halves[s, 1] = low
        left = jnp.concatenate([high, high, low], axis=0)
        right = jnp.concatenate([high, low, high], axis=0)
        state[s, 0] = state[s, 0] + matmul(left, right, ((0,), (0,)))
        left = jnp.concatenate([high, high, low], axis=1)
        right = jnp.concatenate([high, low, high], axis=1)
        state[s, 1] = state[s, 1] + matmul(left, right, ((1,), (1,)))
    for save in saves:
        save.start()

    row = lax.broadcasted_iota(jnp.int32, (edge, edge), 0)
    col = lax.broadcasted_iota(jnp.int32, (edge, edge), 1)
    identity = (row == col).astype(F32)
    count = REFRESH_MOST * 2

    def less_middle(old):
        small = [(1.25 - MIDDLE) * identity - 0.25 * x for x in old]
        for middle in (MIDDLE, MIDDLE**2):
            high = [x.astype(BF16) for x in small]
            small = [2.0 * middle * x + matmul(h, h) for x, h in zip(small, high)]
        return small

    starts = []
    for b in range(count):
        slot = jnp.maximum(picked[b // 2], 0)
        shifted = state[slot, b % 2] + EPSILON * identity
        norm = jnp.sqrt(jnp.sum(shifted * shifted, axis=(0, 1), keepdims=True))
        scaled = shifted / norm
        current[b] = (5.0 * identity - scaled) * 0.25 / jnp.sqrt(jnp.sqrt(norm))
        starts.append(scaled)
    fourth = less_middle(starts)
    for b in range(count):
        moving[b] = MIDDLE**4 * starts[b] + product(split(fourth[b]), split(starts[b]))

    def step(iteration, carry):
        old = [moving[b] for b in range(count)]
        halves = [split(x) for x in old]
        small = [(1.25 - MIDDLE) * identity - 0.25 * x for x in old]
        high = [x.astype(BF16) for x in small]
        small = [2.0 * MIDDLE * x + matmul(h, h) for x, h in zip(small, high)]
        for b in range(count):
            x = current[b]
            current[b] = 1.25 * x - 0.25 * product(split(x), halves[b])
        high = [x.astype(BF16) for x in small]
        fourth = [2.0 * MIDDLE**2 * x + matmul(h, h) for x, h in zip(small, high)]
        for b in range(count):
            moving[b] = MIDDLE**4 * old[b] + product(split(fourth[b]), halves[b])
        return carry

    lax.fori_loop(1, ITERS - 1, step, 0, unroll=2)
    load_roots.wait()
    for b in range(count):
        x = current[b]
        final = (1.25 * x - 0.25 * product(split(x), split(moving[b]))).astype(BF16)

        @pl.when(picked[b // 2] >= 0)
        def _():
            roots[picked[b // 2], b % 2] = final

    save_roots = pltpu.make_async_copy(roots, roots_out, roots_sems.at[1])
    save_roots.start()

    for s in range(slots):
        high, low = halves[s, 0], halves[s, 1]
        left = roots[s, 0]
        right = roots[s, 1]
        first = matmul(
            jnp.concatenate([high, low], axis=0),
            jnp.concatenate([right, right], axis=0),
            ((0,), (0,)),
        )
        fh, fl = split(first)
        precond = matmul(
            jnp.concatenate([left, left], axis=1), jnp.concatenate([fh, fl], axis=0)
        )
        block = high.astype(F32) + low.astype(F32)
        block_sum = jnp.sum(block * block, axis=(0, 1), keepdims=True)
        precond_sum = jnp.sum(precond * precond, axis=(0, 1), keepdims=True)
        ratio = jnp.sqrt(block_sum / (precond_sum + 1e-06))
        code(precond * ratio, results, s)
    for s in range(slots):

        @pl.when(table[s] >= 0)
        def _():
            out_ref[table[s]] = results[s]

    save_roots.wait()
    for save in saves:
        save.wait()


def home_kernel(edge, owner_ref, in_hbm, out_hbm, blocks, values, sems):
    dp_index, mp_index = lax.axis_index("dp"), lax.axis_index("mp")
    col_blocks = out_hbm.shape[1] // edge
    loads, saves = [], []
    for j in range(blocks.shape[0]):
        owner = owner_ref[dp_index, j, mp_index]
        top, left = (j // col_blocks) * edge, (j % col_blocks) * edge
        loads.append(pltpu.make_async_copy(in_hbm.at[owner], blocks.at[j], sems.at[0, j]))
        saves.append(
            pltpu.make_async_copy(
                values.at[j], out_hbm.at[top : top + edge, left : left + edge], sems.at[1, j]
            )
        )
    for load in loads:
        load.start()
    for j, load in enumerate(loads):
        load.wait()
        whole, unit = decode(blocks, j, edge)
        values[j] = whole * unit
        saves[j].start()
    for save in saves:
        save.wait()


def body(acts, cotangent, factors, roots, owner_of, slot_of, refresh_ids):
    dp_count = lax.axis_size("dp")
    mp_count = lax.axis_size("mp")
    edge = factors.shape[-1]
    slots = factors.shape[1]
    tokens = acts.shape[0]
    row_count = acts.shape[1] // dp_count
    slab = cotangent.shape[1]
    ways = math.isqrt(mp_count)
    rows = 2 * edge // ways
    half = rows // 2
    owner_of = owner_of.transpose(0, 2, 1)
    slot_of = slot_of.transpose(0, 2, 1)

    smem = pl.BlockSpec(memory_space=SMEM)
    vmem = pl.BlockSpec(memory_space=VMEM)
    hbm = pl.BlockSpec(memory_space=pl.ANY)

    around = [(i, (i + (2, -2)[i % 2]) % dp_count) for i in range(dp_count)]
    swap = [(i, i ^ 1) for i in range(dp_count)]

    def along_y(x, k):
        return lax.ppermute(x, "mp", [(i, (i + ways * k) % mp_count) for i in range(mp_count)])

    def along_x(x, k):
        return lax.ppermute(
            x, "mp", [(i, (i // ways) * ways + (i + k) % ways) for i in range(mp_count)]
        )

    def swapped(x):
        return lax.ppermute(x, "dp", swap)

    def ring(x):
        return lax.ppermute(x, "dp", around)

    picked = pl.pallas_call(
        functools.partial(pick_kernel, edge),
        out_shape=jax.ShapeDtypeStruct((dp_count, rows, tokens), BF16),
        in_specs=[vmem],
        out_specs=vmem,
    )(acts)

    strips = pl.pallas_call(
        functools.partial(strip_kernel, edge),
        out_shape=jax.ShapeDtypeStruct((mp_count, slab // mp_count, tokens), BF16),
        in_specs=[vmem],
        out_specs=vmem,
    )(cotangent)
    strips = lax.all_to_all(strips, "mp", split_axis=0, concat_axis=0, tiled=True)
    strips = strips.reshape(slab, tokens)
    both = jnp.stack([strips, swapped(strips)])
    first = ring(both)
    second = ring(first)
    own = lax.all_to_all(picked, "dp", split_axis=0, concat_axis=0, tiled=True)
    own, both, first, second = lax.optimization_barrier((own, both, first, second))
    by_y, by_x = own[:, :half], own[:, half:]
    near = [along_y(by_y, 1), along_y(by_y, ways - 1), along_x(by_x, 1), along_x(by_x, ways - 1)]
    third = ring(second)
    near, third, by_y, by_x = lax.optimization_barrier((near, third, by_y, by_x))
    far = [along_y(by_y, ways // 2), along_x(by_x, ways // 2)]
    others = [near[0], far[0], near[1], near[2], far[1], near[3]]
    gathered = [both]
    for part in (first, second, third):
        gathered += [part, swapped(part)]
    gathered.append(ring(third))

    depth = edge // mp_count
    outgoing = pl.pallas_call(
        functools.partial(gradient_kernel, edge, slots),
        out_shape=jax.ShapeDtypeStruct((mp_count, slots * depth + PAD, edge), jnp.int16),
        in_specs=[smem, smem, hbm] + [hbm] * len(others + gathered),
        out_specs=vmem,
        scratch_shapes=[
            VMEM((dp_count, row_count, tokens), BF16),
            VMEM((dp_count // 2, 2, slab, tokens), BF16),
            VMEM((mp_count, PAD, edge), F32),
            pltpu.SemaphoreType.DMA((2 + len(others + gathered),)),
        ],
        compiler_params=pltpu.CompilerParams(vmem_limit_bytes=60 * 1024 * 1024),
    )(owner_of, slot_of, own, *others, *gathered)
    incoming = lax.all_to_all(outgoing, "mp", split_axis=0, concat_axis=0, tiled=True)

    count = REFRESH_MOST * 2
    factors_next, roots_next, homeward = pl.pallas_call(
        owner_kernel,
        out_shape=(
            jax.ShapeDtypeStruct(factors.shape[1:], F32),
            jax.ShapeDtypeStruct(roots.shape[1:], BF16),
            jax.ShapeDtypeStruct((mp_count, edge + PAD, edge), jnp.int16),
        ),
        in_specs=[smem, smem, smem, vmem, hbm, hbm],
        out_specs=(hbm, hbm, vmem),
        scratch_shapes=[
            VMEM(factors.shape[1:], F32),
            VMEM(roots.shape[1:], BF16),
            VMEM((mp_count, PAD, edge), F32),
            VMEM((slots, 2, edge, edge), BF16),
            VMEM((slots, edge + PAD, edge), jnp.int16),
            VMEM((count, edge, edge), F32),
            VMEM((count, edge, edge), F32),
            SMEM((slots + 1,), jnp.int32),
            SMEM((REFRESH_MOST + 1,), jnp.int32),
            pltpu.SemaphoreType.DMA((slots,)),
            pltpu.SemaphoreType.DMA((slots,)),
            pltpu.SemaphoreType.DMA((2,)),
        ],
        compiler_params=pltpu.CompilerParams(vmem_limit_bytes=28 * 1024 * 1024),
    )(owner_of, slot_of, refresh_ids, incoming, factors[0], roots[0])
    returned = lax.all_to_all(homeward, "mp", split_axis=0, concat_axis=0, tiled=True)

    local_blocks = owner_of.shape[1]
    direction = pl.pallas_call(
        functools.partial(home_kernel, edge),
        out_shape=jax.ShapeDtypeStruct((row_count, slab), F32),
        in_specs=[smem, hbm],
        out_specs=hbm,
        scratch_shapes=[
            VMEM((local_blocks, edge + PAD, edge), jnp.int16),
            VMEM((local_blocks, edge, edge), F32),
            pltpu.SemaphoreType.DMA((2, local_blocks)),
        ],
    )(owner_of, returned)
    return (direction, factors_next[None], roots_next[None])


def solution(mesh):
    in_specs = (
        P("dp", None),
        P("dp", "mp"),
        P("dp", "mp", None, None, None),
        P("dp", "mp", None, None, None),
        P(),
        P(),
        P(),
    )
    out_specs = (P("dp", "mp"), P("dp", "mp", None, None, None), P("dp", "mp", None, None, None))
    return jax.shard_map(body, mesh=mesh, in_specs=in_specs, out_specs=out_specs, check_vma=False)
```

```python
import functools
import math

import jax
import jax.numpy as jnp
from jax import lax
from jax.experimental import pallas as pl
from jax.experimental.pallas import tpu as pltpu
from jax.sharding import PartitionSpec as P

ITERS = 10
REFRESH_MOST = 2
EPSILON = 0.1
PAD = 16
TOP_BITS = 14
MIDDLE = 1.125
F32 = jnp.float32
BF16 = jnp.bfloat16
VMEM = pltpu.VMEM
SMEM = pltpu.SMEM


def matmul(left, right, dims=((1,), (0,))):
    return lax.dot_general(left, right, (dims, ((), ())), preferred_element_type=F32)


def split(x):
    high = x.astype(BF16)
    return high, (x - high.astype(F32)).astype(BF16)


def product(left, right):
    lh, ll = left
    rh, rl = right
    return matmul(
        jnp.concatenate([lh, lh, ll], axis=1), jnp.concatenate([rh, rl, rh], axis=0)
    )


def quantized(values, shift):
    scaled = jnp.clip(jnp.round(values * jnp.exp2(shift)), -32767.0, 32767.0)
    return scaled.astype(jnp.int32).astype(jnp.int16)


def code(block, out_ref, place):
    edge = block.shape[0]
    most = jnp.maximum(jnp.max(jnp.abs(block), axis=(0, 1), keepdims=True), 1e-30)
    shift = TOP_BITS - jnp.floor(jnp.log2(most))
    out_ref[place, :edge, :] = quantized(block, shift)
    out_ref[place, edge:, :] = jnp.broadcast_to(
        shift.astype(jnp.int32), (PAD, block.shape[1])
    ).astype(jnp.int16)


def decode(in_ref, place, edge):
    whole = in_ref[place, :edge, :].astype(jnp.int32).astype(F32)
    shift = in_ref[place, edge:, :].astype(jnp.int32).astype(F32)[:1, :]
    return whole, jnp.exp2(-shift)


def position(ways):
    mp_index = lax.axis_index("mp")
    return mp_index // ways, lax.rem(mp_index, ways)


def pick_kernel(edge, acts_ref, out_ref):
    parts, rows, tokens = out_ref.shape
    half = rows // 2
    width = acts_ref.shape[1] // parts
    lanes = 128
    row = lax.broadcasted_iota(jnp.int32, (half, lanes), 0)
    col = lax.broadcasted_iota(jnp.int32, (half, lanes), 1)
    for side in range(2):
        first = position(edge // half)[side] * half
        group = first // lanes
        inside = lax.rem(first, lanes)
        chosen = (col == row + inside).astype(F32).astype(BF16)
        for part in range(parts):
            start = pl.multiple_of(part * width + side * edge + group * lanes, lanes)
            piece = acts_ref[:, pl.ds(start, lanes)]
            out_ref[part, side * half : (side + 1) * half, :] = matmul(
                chosen, piece, ((1,), (1,))
            ).astype(BF16)


def strip_kernel(edge, cot_ref, out_ref):
    owners, rows, lanes = out_ref.shape
    blocks = cot_ref.shape[1] // edge
    depth = rows // blocks
    row = lax.broadcasted_iota(jnp.int32, (lanes, lanes), 0)
    col = lax.broadcasted_iota(jnp.int32, (lanes, lanes), 1)
    identity = (row == col).astype(F32).astype(BF16)
    for chunk in range(cot_ref.shape[1] // lanes):
        piece = cot_ref[:, chunk * lanes : (chunk + 1) * lanes]
        turned = matmul(identity, piece, ((1,), (1,))).astype(BF16)
        block, first = divmod(chunk * lanes, edge)
        for k in range(lanes // depth):
            out_ref[first // depth + k, block * depth : (block + 1) * depth, :] = turned[
                k * depth : (k + 1) * depth
            ]


def gradient_kernel(edge, slots, owner_ref, place_ref, own_ref, *refs):
    out_ref, left, shifts = refs[-3:]
    times, rows, tokens = own_ref.shape
    chips = times // 2
    rights, others = refs[-3 - chips : -3], refs[: -3 - chips]
    half = rows // 2
    ways = edge // half
    sources = ways * ways
    depth = edge // sources
    dp_index = lax.axis_index("dp")
    for side, place in enumerate(position(ways)):
        for away in range(ways):
            part = lax.rem(place + (ways - away), ways)
            top = pl.multiple_of(side * edge + part * half, half)
            if away == 0:
                left[:, pl.ds(top, half), :] = own_ref[:, side * half : (side + 1) * half, :]
            else:
                left[:, pl.ds(top, half), :] = others[side * (ways - 1) + away - 1][...]
    shifts[...] = jnp.zeros_like(shifts)
    total = left.shape[1]
    when = token_groups(dp_index, chips)
    left = jnp.concatenate([left[t] for t in when], axis=1)
    slab = rights[0].shape[1]
    col_blocks = slab // (sources * depth)
    for chunk in range(slab // edge):
        strips = jnp.concatenate(
            [rights[k // 2][k % 2, chunk * edge : (chunk + 1) * edge, :] for k in range(times)],
            axis=1,
        )
        product_t = matmul(strips, left, ((1,), (1,))).reshape(edge // depth, depth, total)
        for row_block in range(total // edge):
            values = product_t[:, :, row_block * edge : (row_block + 1) * edge]
            most = jnp.max(jnp.abs(values), axis=(1, 2), keepdims=True)
            shift = TOP_BITS - jnp.floor(jnp.log2(jnp.maximum(most, 1e-30)))
            coded = quantized(values, shift)
            for k in range(edge // depth):
                m, col_block = divmod(chunk * (edge // depth) + k, col_blocks)
                j = row_block * col_blocks + col_block
                owner, place = owner_ref[dp_index, j, m], place_ref[dp_index, j, m]
                top = pl.multiple_of(place * depth, depth)
                out_ref[owner, pl.ds(top, depth), :] = coded[k]
                shifts[owner, pl.ds(place, 1), :] = jnp.broadcast_to(shift[k], (1, edge))
    out_ref[:, slots * depth :, :] = shifts[...].astype(jnp.int32).astype(jnp.int16)


def token_groups(dp_index, chips):
    chip, core = dp_index // 2, lax.rem(dp_index, 2)
    away = 1 - 2 * core
    groups = [2 * chip + core, 2 * chip + 1 - core]
    for step in range(1, chips // 2 + 1):
        for side in (-1, 1)[: 2 if step < chips // 2 else 1]:
            first = core if side < 0 else 1 - core
            base = 2 * lax.rem(chip + side * step * away + chips, chips)
            groups += [base + first, base + 1 - first]
    return groups


def owner_kernel(
    owner_ref,
    place_ref,
    fresh_ref,
    in_ref,
    factors_ref,
    roots_ref,
    factors_out,
    roots_out,
    out_ref,
    state,
    roots,
    units,
    halves,
    results,
    moving,
    current,
    table,
    picked,
    state_sems,
    roots_sem,
):
    slots, _, edge, _ = state.shape
    local_blocks, sources = owner_ref.shape[1:]
    dp_index, mp_index = lax.axis_index("dp"), lax.axis_index("mp")
    saves = [
        pltpu.make_async_copy(state.at[s], factors_out.at[s], state_sems.at[s])
        for s in range(slots)
    ]

    for s in range(slots + 1):
        table[s] = -1
    for s in range(REFRESH_MOST + 1):
        picked[s] = -1

    def place_source(m, carry):
        for j in range(local_blocks):
            held = owner_ref[dp_index, j, m] == mp_index
            table[jnp.where(held, place_ref[dp_index, j, m], slots)] = m
        return carry

    lax.fori_loop(0, sources, place_source, 0)

    def place_fresh(i, count):
        block = fresh_ref[dp_index, i]
        m, j = block // local_blocks, lax.rem(block, local_blocks)
        held = owner_ref[dp_index, j, m] == mp_index
        picked[jnp.where(held, count, REFRESH_MOST)] = place_ref[dp_index, j, m]
        return count + held.astype(jnp.int32)

    lax.fori_loop(0, fresh_ref.shape[1], place_fresh, jnp.int32(0))

    depth = edge // sources
    units[...] = jnp.exp2(-in_ref[:, slots * depth :, :].astype(jnp.int32).astype(F32))
    for s in range(slots):
        whole = in_ref[:, s * depth : (s + 1) * depth, :].astype(jnp.int32).astype(F32)
        block = jnp.where(table[s] >= 0, whole * units[:, s : s + 1, :], 0.0)
        high, low = split(block.reshape(edge, edge))
        halves[s, 0] = high
        halves[s, 1] = low
        left = jnp.concatenate([high, high, low], axis=0)
        right = jnp.concatenate([high, low, high], axis=0)
        state[s, 0] = factors_ref[s, 0] + matmul(left, right, ((0,), (0,)))
        left = jnp.concatenate([high, high, low], axis=1)
        right = jnp.concatenate([high, low, high], axis=1)
        state[s, 1] = factors_ref[s, 1] + matmul(left, right, ((1,), (1,)))
        saves[s].start()
    roots[...] = roots_ref[...]

    row = lax.broadcasted_iota(jnp.int32, (edge, edge), 0)
    col = lax.broadcasted_iota(jnp.int32, (edge, edge), 1)
    identity = (row == col).astype(F32)
    count = REFRESH_MOST * 2

    def less_middle(old):
        small = [(1.25 - MIDDLE) * identity - 0.25 * x for x in old]
        for middle in (MIDDLE, MIDDLE**2):
            high = [x.astype(BF16) for x in small]
            small = [2.0 * middle * x + matmul(h, h) for x, h in zip(small, high)]
        return small

    starts = []
    for b in range(count):
        slot = jnp.maximum(picked[b // 2], 0)
        shifted = state[slot, b % 2] + EPSILON * identity
        norm = jnp.sqrt(jnp.sum(shifted * shifted, axis=(0, 1), keepdims=True))
        scaled = shifted / norm
        current[b] = (5.0 * identity - scaled) * 0.25 / jnp.sqrt(jnp.sqrt(norm))
        starts.append(scaled)
    fourth = less_middle(starts)
    for b in range(count):
        moving[b] = MIDDLE**4 * starts[b] + product(split(fourth[b]), split(starts[b]))

    def step(iteration, carry):
        old = [moving[b] for b in range(count)]
        halves = [split(x) for x in old]
        small = [(1.25 - MIDDLE) * identity - 0.25 * x for x in old]
        high = [x.astype(BF16) for x in small]
        small = [2.0 * MIDDLE * x + matmul(h, h) for x, h in zip(small, high)]
        for b in range(count):
            x = current[b]
            current[b] = 1.25 * x - 0.25 * product(split(x), halves[b])
        high = [x.astype(BF16) for x in small]
        fourth = [2.0 * MIDDLE**2 * x + matmul(h, h) for x, h in zip(small, high)]
        for b in range(count):
            moving[b] = MIDDLE**4 * old[b] + product(split(fourth[b]), halves[b])
        return carry

    lax.fori_loop(1, ITERS - 1, step, 0, unroll=2)
    for b in range(count):
        x = current[b]
        final = (1.25 * x - 0.25 * product(split(x), split(moving[b]))).astype(BF16)

        @pl.when(picked[b // 2] >= 0)
        def _():
            roots[picked[b // 2], b % 2] = final

    save_roots = pltpu.make_async_copy(roots, roots_out, roots_sem)
    save_roots.start()

    for s in range(slots):
        high, low = halves[s, 0], halves[s, 1]
        left = roots[s, 0]
        right = roots[s, 1]
        first = matmul(
            jnp.concatenate([high, low], axis=0),
            jnp.concatenate([right, right], axis=0),
            ((0,), (0,)),
        )
        fh, fl = split(first)
        precond = matmul(
            jnp.concatenate([left, left], axis=1), jnp.concatenate([fh, fl], axis=0)
        )
        block = high.astype(F32) + low.astype(F32)
        block_sum = jnp.sum(block * block, axis=(0, 1), keepdims=True)
        precond_sum = jnp.sum(precond * precond, axis=(0, 1), keepdims=True)
        ratio = jnp.sqrt(block_sum / (precond_sum + 1e-06))
        code(precond * ratio, results, s)
    for s in range(slots):

        @pl.when(table[s] >= 0)
        def _():
            out_ref[table[s]] = results[s]

    save_roots.wait()
    for save in saves:
        save.wait()


def home_kernel(edge, owner_ref, in_hbm, out_hbm, blocks, values, sems):
    dp_index, mp_index = lax.axis_index("dp"), lax.axis_index("mp")
    col_blocks = out_hbm.shape[1] // edge
    loads, saves = [], []
    for j in range(blocks.shape[0]):
        owner = owner_ref[dp_index, j, mp_index]
        top, left = (j // col_blocks) * edge, (j % col_blocks) * edge
        loads.append(pltpu.make_async_copy(in_hbm.at[owner], blocks.at[j], sems.at[0, j]))
        saves.append(
            pltpu.make_async_copy(
                values.at[j], out_hbm.at[top : top + edge, left : left + edge], sems.at[1, j]
            )
        )
    for load in loads:
        load.start()
    for j, load in enumerate(loads):
        load.wait()
        whole, unit = decode(blocks, j, edge)
        values[j] = whole * unit
        saves[j].start()
    for save in saves:
        save.wait()


def body(acts, cotangent, factors, roots, owner_of, slot_of, refresh_ids):
    dp_count = lax.axis_size("dp")
    mp_count = lax.axis_size("mp")
    edge = factors.shape[-1]
    slots = factors.shape[1]
    tokens = acts.shape[0]
    row_count = acts.shape[1] // dp_count
    slab = cotangent.shape[1]
    ways = math.isqrt(mp_count)
    rows = 2 * edge // ways
    half = rows // 2
    owner_of = owner_of.transpose(0, 2, 1)
    slot_of = slot_of.transpose(0, 2, 1)

    smem = pl.BlockSpec(memory_space=SMEM)
    vmem = pl.BlockSpec(memory_space=VMEM)
    hbm = pl.BlockSpec(memory_space=pl.ANY)

    around = [(i, (i + (2, -2)[i % 2]) % dp_count) for i in range(dp_count)]
    swap = [(i, i ^ 1) for i in range(dp_count)]

    def along_y(x, k):
        return lax.ppermute(x, "mp", [(i, (i + ways * k) % mp_count) for i in range(mp_count)])

    def along_x(x, k):
        return lax.ppermute(
            x, "mp", [(i, (i // ways) * ways + (i + k) % ways) for i in range(mp_count)]
        )

    def swapped(x):
        return lax.ppermute(x, "dp", swap)

    def ring(x):
        return lax.ppermute(x, "dp", around)

    picked = pl.pallas_call(
        functools.partial(pick_kernel, edge),
        out_shape=jax.ShapeDtypeStruct((dp_count, rows, tokens), BF16),
        in_specs=[vmem],
        out_specs=vmem,
    )(acts)

    strips = pl.pallas_call(
        functools.partial(strip_kernel, edge),
        out_shape=jax.ShapeDtypeStruct((mp_count, slab // mp_count, tokens), BF16),
        in_specs=[vmem],
        out_specs=vmem,
    )(cotangent)
    strips = lax.all_to_all(strips, "mp", split_axis=0, concat_axis=0, tiled=True)
    strips = strips.reshape(slab, tokens)
    picked, strips = lax.optimization_barrier((picked, strips))
    both = jnp.stack([strips, swapped(strips)])
    picked, both = lax.optimization_barrier((picked, both))
    first = ring(both)
    own = lax.all_to_all(picked, "dp", split_axis=0, concat_axis=0, tiled=True)
    own, both, first = lax.optimization_barrier((own, both, first))
    by_y, by_x = own[:, :half], own[:, half:]
    near = [along_y(by_y, 1), along_y(by_y, ways - 1), along_x(by_x, 1), along_x(by_x, ways - 1)]
    second = ring(first)
    third = ring(second)
    near, third, by_y, by_x = lax.optimization_barrier((near, third, by_y, by_x))
    far = [along_y(by_y, ways // 2), along_x(by_x, ways // 2)]
    others = [near[0], far[0], near[1], near[2], far[1], near[3]]
    gathered = [both]
    for part in (first, second, third):
        gathered += [part, swapped(part)]
    gathered.append(ring(third))

    depth = edge // mp_count
    outgoing = pl.pallas_call(
        functools.partial(gradient_kernel, edge, slots),
        out_shape=jax.ShapeDtypeStruct((mp_count, slots * depth + PAD, edge), jnp.int16),
        in_specs=[smem, smem, vmem] + [vmem] * len(others + gathered),
        out_specs=vmem,
        scratch_shapes=[
            VMEM((dp_count, row_count, tokens), BF16),
            VMEM((mp_count, PAD, edge), F32),
        ],
        compiler_params=pltpu.CompilerParams(vmem_limit_bytes=20 * 1024 * 1024),
    )(owner_of, slot_of, own, *others, *gathered)
    incoming = lax.all_to_all(outgoing, "mp", split_axis=0, concat_axis=0, tiled=True)

    count = REFRESH_MOST * 2
    factors_next, roots_next, homeward = pl.pallas_call(
        owner_kernel,
        out_shape=(
            jax.ShapeDtypeStruct(factors.shape[1:], F32),
            jax.ShapeDtypeStruct(roots.shape[1:], BF16),
            jax.ShapeDtypeStruct((mp_count, edge + PAD, edge), jnp.int16),
        ),
        in_specs=[smem, smem, smem, vmem, vmem, vmem],
        out_specs=(hbm, hbm, vmem),
        scratch_shapes=[
            VMEM(factors.shape[1:], F32),
            VMEM(roots.shape[1:], BF16),
            VMEM((mp_count, PAD, edge), F32),
            VMEM((slots, 2, edge, edge), BF16),
            VMEM((slots, edge + PAD, edge), jnp.int16),
            VMEM((count, edge, edge), F32),
            VMEM((count, edge, edge), F32),
            SMEM((slots + 1,), jnp.int32),
            SMEM((REFRESH_MOST + 1,), jnp.int32),
            pltpu.SemaphoreType.DMA((slots,)),
            pltpu.SemaphoreType.DMA,
        ],
        compiler_params=pltpu.CompilerParams(vmem_limit_bytes=28 * 1024 * 1024),
    )(owner_of, slot_of, refresh_ids, incoming, factors[0], roots[0])
    returned = lax.all_to_all(homeward, "mp", split_axis=0, concat_axis=0, tiled=True)

    local_blocks = owner_of.shape[1]
    direction = pl.pallas_call(
        functools.partial(home_kernel, edge),
        out_shape=jax.ShapeDtypeStruct((row_count, slab), F32),
        in_specs=[smem, hbm],
        out_specs=hbm,
        scratch_shapes=[
            VMEM((local_blocks, edge + PAD, edge), jnp.int16),
            VMEM((local_blocks, edge, edge), F32),
            pltpu.SemaphoreType.DMA((2, local_blocks)),
        ],
    )(owner_of, returned)
    return (direction, factors_next[None], roots_next[None])


def solution(mesh):
    in_specs = (
        P("dp", None),
        P("dp", "mp"),
        P("dp", "mp", None, None, None),
        P("dp", "mp", None, None, None),
        P(),
        P(),
        P(),
    )
    out_specs = (P("dp", "mp"), P("dp", "mp", None, None, None), P("dp", "mp", None, None, None))
    return jax.shard_map(body, mesh=mesh, in_specs=in_specs, out_specs=out_specs, check_vma=False)
```

```python
import functools
import math

import jax
import jax.numpy as jnp
from jax import lax
from jax.experimental import pallas as pl
from jax.experimental.pallas import tpu as pltpu
from jax.sharding import PartitionSpec as P

ITERS = 10
REFRESH_MOST = 2
EPSILON = 0.1
PAD = 16
TOP_BITS = 14
MIDDLE = 1.125
F32 = jnp.float32
BF16 = jnp.bfloat16
VMEM = pltpu.VMEM
SMEM = pltpu.SMEM


def matmul(left, right, dims=((1,), (0,))):
    return lax.dot_general(left, right, (dims, ((), ())), preferred_element_type=F32)


def split(x):
    high = x.astype(BF16)
    return high, (x - high.astype(F32)).astype(BF16)


def product(left, right):
    lh, ll = left
    rh, rl = right
    return matmul(
        jnp.concatenate([lh, lh, ll], axis=1), jnp.concatenate([rh, rl, rh], axis=0)
    )


def quantized(values, shift):
    scaled = jnp.clip(jnp.round(values * jnp.exp2(shift)), -32767.0, 32767.0)
    return scaled.astype(jnp.int32).astype(jnp.int16)


def code(block, out_ref, place):
    edge = block.shape[0]
    most = jnp.maximum(jnp.max(jnp.abs(block), axis=(0, 1), keepdims=True), 1e-30)
    shift = TOP_BITS - jnp.floor(jnp.log2(most))
    out_ref[place, :edge, :] = quantized(block, shift)
    out_ref[place, edge:, :] = jnp.broadcast_to(
        shift.astype(jnp.int32), (PAD, block.shape[1])
    ).astype(jnp.int16)


def decode(in_ref, place, edge):
    whole = in_ref[place, :edge, :].astype(jnp.int32).astype(F32)
    shift = in_ref[place, edge:, :].astype(jnp.int32).astype(F32)[:1, :]
    return whole, jnp.exp2(-shift)


def position(ways):
    mp_index = lax.axis_index("mp")
    return mp_index // ways, lax.rem(mp_index, ways)


def pick_kernel(edge, acts_ref, out_ref):
    parts, rows, tokens = out_ref.shape
    half = rows // 2
    width = acts_ref.shape[1] // parts
    lanes = 128
    row = lax.broadcasted_iota(jnp.int32, (half, lanes), 0)
    col = lax.broadcasted_iota(jnp.int32, (half, lanes), 1)
    for side in range(2):
        first = position(edge // half)[side] * half
        group = first // lanes
        inside = lax.rem(first, lanes)
        chosen = (col == row + inside).astype(F32).astype(BF16)
        for part in range(parts):
            start = pl.multiple_of(part * width + side * edge + group * lanes, lanes)
            piece = acts_ref[:, pl.ds(start, lanes)]
            out_ref[part, side * half : (side + 1) * half, :] = matmul(
                chosen, piece, ((1,), (1,))
            ).astype(BF16)


def strip_kernel(edge, cot_ref, out_ref):
    owners, rows, lanes = out_ref.shape
    blocks = cot_ref.shape[1] // edge
    depth = rows // blocks
    row = lax.broadcasted_iota(jnp.int32, (lanes, lanes), 0)
    col = lax.broadcasted_iota(jnp.int32, (lanes, lanes), 1)
    identity = (row == col).astype(F32).astype(BF16)
    for chunk in range(cot_ref.shape[1] // lanes):
        piece = cot_ref[:, chunk * lanes : (chunk + 1) * lanes]
        turned = matmul(identity, piece, ((1,), (1,))).astype(BF16)
        block, first = divmod(chunk * lanes, edge)
        for k in range(lanes // depth):
            out_ref[first // depth + k, block * depth : (block + 1) * depth, :] = turned[
                k * depth : (k + 1) * depth
            ]


def gradient_kernel(edge, slots, owner_ref, place_ref, own_ref, *refs):
    out_ref, left, shifts = refs[-3:]
    times, rows, tokens = own_ref.shape
    chips = times // 2
    rights, others = refs[-3 - chips : -3], refs[: -3 - chips]
    half = rows // 2
    ways = edge // half
    sources = ways * ways
    depth = edge // sources
    dp_index = lax.axis_index("dp")
    for side, place in enumerate(position(ways)):
        for away in range(ways):
            part = lax.rem(place + (ways - away), ways)
            top = pl.multiple_of(side * edge + part * half, half)
            if away == 0:
                left[:, pl.ds(top, half), :] = own_ref[:, side * half : (side + 1) * half, :]
            else:
                left[:, pl.ds(top, half), :] = others[side * (ways - 1) + away - 1][...]
    shifts[...] = jnp.zeros_like(shifts)
    total = left.shape[1]
    when = token_groups(dp_index, chips)
    left = jnp.concatenate([left[t] for t in when], axis=1)
    slab = rights[0].shape[1]
    col_blocks = slab // (sources * depth)
    for chunk in range(slab // edge):
        strips = jnp.concatenate(
            [rights[k // 2][k % 2, chunk * edge : (chunk + 1) * edge, :] for k in range(times)],
            axis=1,
        )
        product_t = matmul(strips, left, ((1,), (1,))).reshape(edge // depth, depth, total)
        for row_block in range(total // edge):
            values = product_t[:, :, row_block * edge : (row_block + 1) * edge]
            most = jnp.max(jnp.abs(values), axis=(1, 2), keepdims=True)
            shift = TOP_BITS - jnp.floor(jnp.log2(jnp.maximum(most, 1e-30)))
            coded = quantized(values, shift)
            for k in range(edge // depth):
                m, col_block = divmod(chunk * (edge // depth) + k, col_blocks)
                j = row_block * col_blocks + col_block
                owner, place = owner_ref[dp_index, j, m], place_ref[dp_index, j, m]
                top = pl.multiple_of(place * depth, depth)
                out_ref[owner, pl.ds(top, depth), :] = coded[k]
                shifts[owner, pl.ds(place, 1), :] = jnp.broadcast_to(shift[k], (1, edge))
    out_ref[:, slots * depth :, :] = shifts[...].astype(jnp.int32).astype(jnp.int16)


def token_groups(dp_index, chips):
    chip, core = dp_index // 2, lax.rem(dp_index, 2)
    away = 1 - 2 * core
    groups = [2 * chip + core, 2 * chip + 1 - core]
    for step in range(1, chips // 2 + 1):
        for side in (-1, 1)[: 2 if step < chips // 2 else 1]:
            first = core if side < 0 else 1 - core
            base = 2 * lax.rem(chip + side * step * away + chips, chips)
            groups += [base + first, base + 1 - first]
    return groups


def owner_kernel(
    owner_ref,
    place_ref,
    fresh_ref,
    in_ref,
    factors_ref,
    roots_ref,
    factors_out,
    roots_out,
    out_ref,
    state,
    roots,
    units,
    halves,
    results,
    moving,
    current,
    table,
    picked,
    state_sems,
    roots_sem,
):
    slots, _, edge, _ = state.shape
    local_blocks, sources = owner_ref.shape[1:]
    dp_index, mp_index = lax.axis_index("dp"), lax.axis_index("mp")
    saves = [
        pltpu.make_async_copy(state.at[s], factors_out.at[s], state_sems.at[s])
        for s in range(slots)
    ]

    for s in range(slots + 1):
        table[s] = -1
    for s in range(REFRESH_MOST + 1):
        picked[s] = -1

    def place_source(m, carry):
        for j in range(local_blocks):
            held = owner_ref[dp_index, j, m] == mp_index
            table[jnp.where(held, place_ref[dp_index, j, m], slots)] = m
        return carry

    lax.fori_loop(0, sources, place_source, 0)

    def place_fresh(i, count):
        block = fresh_ref[dp_index, i]
        m, j = block // local_blocks, lax.rem(block, local_blocks)
        held = owner_ref[dp_index, j, m] == mp_index
        picked[jnp.where(held, count, REFRESH_MOST)] = place_ref[dp_index, j, m]
        return count + held.astype(jnp.int32)

    lax.fori_loop(0, fresh_ref.shape[1], place_fresh, jnp.int32(0))

    depth = edge // sources
    units[...] = jnp.exp2(-in_ref[:, slots * depth :, :].astype(jnp.int32).astype(F32))
    for s in range(slots):
        whole = in_ref[:, s * depth : (s + 1) * depth, :].astype(jnp.int32).astype(F32)
        block = jnp.where(table[s] >= 0, whole * units[:, s : s + 1, :], 0.0)
        high, low = split(block.reshape(edge, edge))
        halves[s, 0] = high
        halves[s, 1] = low
        left = jnp.concatenate([high, high, low], axis=0)
        right = jnp.concatenate([high, low, high], axis=0)
        state[s, 0] = factors_ref[s, 0] + matmul(left, right, ((0,), (0,)))
        left = jnp.concatenate([high, high, low], axis=1)
        right = jnp.concatenate([high, low, high], axis=1)
        state[s, 1] = factors_ref[s, 1] + matmul(left, right, ((1,), (1,)))
        saves[s].start()
    roots[...] = roots_ref[...]

    row = lax.broadcasted_iota(jnp.int32, (edge, edge), 0)
    col = lax.broadcasted_iota(jnp.int32, (edge, edge), 1)
    identity = (row == col).astype(F32)
    count = REFRESH_MOST * 2

    def less_middle(old):
        small = [(1.25 - MIDDLE) * identity - 0.25 * x for x in old]
        for middle in (MIDDLE, MIDDLE**2):
            high = [x.astype(BF16) for x in small]
            small = [2.0 * middle * x + matmul(h, h) for x, h in zip(small, high)]
        return small

    starts = []
    for b in range(count):
        slot = jnp.maximum(picked[b // 2], 0)
        shifted = state[slot, b % 2] + EPSILON * identity
        norm = jnp.sqrt(jnp.sum(shifted * shifted, axis=(0, 1), keepdims=True))
        scaled = shifted / norm
        current[b] = (5.0 * identity - scaled) * 0.25 / jnp.sqrt(jnp.sqrt(norm))
        starts.append(scaled)
    fourth = less_middle(starts)
    for b in range(count):
        moving[b] = MIDDLE**4 * starts[b] + product(split(fourth[b]), split(starts[b]))

    def step(iteration, carry):
        old = [moving[b] for b in range(count)]
        halves = [split(x) for x in old]
        small = [(1.25 - MIDDLE) * identity - 0.25 * x for x in old]
        high = [x.astype(BF16) for x in small]
        small = [2.0 * MIDDLE * x + matmul(h, h) for x, h in zip(small, high)]
        for b in range(count):
            x = current[b]
            current[b] = 1.25 * x - 0.25 * product(split(x), halves[b])
        high = [x.astype(BF16) for x in small]
        fourth = [2.0 * MIDDLE**2 * x + matmul(h, h) for x, h in zip(small, high)]
        for b in range(count):
            moving[b] = MIDDLE**4 * old[b] + product(split(fourth[b]), halves[b])
        return carry

    lax.fori_loop(1, ITERS - 1, step, 0, unroll=2)
    for b in range(count):
        x = current[b]
        final = (1.25 * x - 0.25 * product(split(x), split(moving[b]))).astype(BF16)

        @pl.when(picked[b // 2] >= 0)
        def _():
            roots[picked[b // 2], b % 2] = final

    save_roots = pltpu.make_async_copy(roots, roots_out, roots_sem)
    save_roots.start()

    for s in range(slots):
        high, low = halves[s, 0], halves[s, 1]
        left = roots[s, 0]
        right = roots[s, 1]
        first = matmul(
            jnp.concatenate([high, low], axis=0),
            jnp.concatenate([right, right], axis=0),
            ((0,), (0,)),
        )
        fh, fl = split(first)
        precond = matmul(
            jnp.concatenate([left, left], axis=1), jnp.concatenate([fh, fl], axis=0)
        )
        block = high.astype(F32) + low.astype(F32)
        block_sum = jnp.sum(block * block, axis=(0, 1), keepdims=True)
        precond_sum = jnp.sum(precond * precond, axis=(0, 1), keepdims=True)
        ratio = jnp.sqrt(block_sum / (precond_sum + 1e-06))
        code(precond * ratio, results, s)
    for s in range(slots):

        @pl.when(table[s] >= 0)
        def _():
            out_ref[table[s]] = results[s]

    save_roots.wait()
    for save in saves:
        save.wait()


def home_kernel(edge, owner_ref, in_ref, out_hbm, values, sems):
    dp_index, mp_index = lax.axis_index("dp"), lax.axis_index("mp")
    col_blocks = out_hbm.shape[1] // edge
    saves = []
    for j in range(values.shape[0]):
        top, left = (j // col_blocks) * edge, (j % col_blocks) * edge
        whole, unit = decode(in_ref, owner_ref[dp_index, j, mp_index], edge)
        values[j] = whole * unit
        saves.append(
            pltpu.make_async_copy(
                values.at[j], out_hbm.at[top : top + edge, left : left + edge], sems.at[j]
            )
        )
        saves[j].start()
    for save in saves:
        save.wait()


def body(acts, cotangent, factors, roots, owner_of, slot_of, refresh_ids):
    dp_count = lax.axis_size("dp")
    mp_count = lax.axis_size("mp")
    edge = factors.shape[-1]
    slots = factors.shape[1]
    tokens = acts.shape[0]
    row_count = acts.shape[1] // dp_count
    slab = cotangent.shape[1]
    ways = math.isqrt(mp_count)
    rows = 2 * edge // ways
    half = rows // 2
    owner_of = owner_of.transpose(0, 2, 1)
    slot_of = slot_of.transpose(0, 2, 1)

    smem = pl.BlockSpec(memory_space=SMEM)
    vmem = pl.BlockSpec(memory_space=VMEM)
    hbm = pl.BlockSpec(memory_space=pl.ANY)

    around = [(i, (i + (2, -2)[i % 2]) % dp_count) for i in range(dp_count)]
    swap = [(i, i ^ 1) for i in range(dp_count)]

    def along_y(x, k):
        return lax.ppermute(x, "mp", [(i, (i + ways * k) % mp_count) for i in range(mp_count)])

    def along_x(x, k):
        return lax.ppermute(
            x, "mp", [(i, (i // ways) * ways + (i + k) % ways) for i in range(mp_count)]
        )

    def swapped(x):
        return lax.ppermute(x, "dp", swap)

    def ring(x):
        return lax.ppermute(x, "dp", around)

    picked = pl.pallas_call(
        functools.partial(pick_kernel, edge),
        out_shape=jax.ShapeDtypeStruct((dp_count, rows, tokens), BF16),
        in_specs=[vmem],
        out_specs=vmem,
    )(acts)

    strips = pl.pallas_call(
        functools.partial(strip_kernel, edge),
        out_shape=jax.ShapeDtypeStruct((mp_count, slab // mp_count, tokens), BF16),
        in_specs=[vmem],
        out_specs=vmem,
    )(cotangent)
    strips = lax.all_to_all(strips, "mp", split_axis=0, concat_axis=0, tiled=True)
    strips = strips.reshape(slab, tokens)
    picked, strips = lax.optimization_barrier((picked, strips))
    both = jnp.stack([strips, swapped(strips)])
    picked, both = lax.optimization_barrier((picked, both))
    first = ring(both)
    own = lax.all_to_all(picked, "dp", split_axis=0, concat_axis=0, tiled=True)
    own, both, first = lax.optimization_barrier((own, both, first))
    by_y, by_x = own[:, :half], own[:, half:]
    near = [along_y(by_y, 1), along_y(by_y, ways - 1), along_x(by_x, 1), along_x(by_x, ways - 1)]
    second = ring(first)
    third = ring(second)
    near, second, by_y, by_x = lax.optimization_barrier((near, second, by_y, by_x))
    far = [along_y(by_y, ways // 2), along_x(by_x, ways // 2)]
    others = [near[0], far[0], near[1], near[2], far[1], near[3]]
    gathered = [both]
    for part in (first, second, third):
        gathered += [part, swapped(part)]
    gathered.append(ring(third))

    depth = edge // mp_count
    outgoing = pl.pallas_call(
        functools.partial(gradient_kernel, edge, slots),
        out_shape=jax.ShapeDtypeStruct((mp_count, slots * depth + PAD, edge), jnp.int16),
        in_specs=[smem, smem, vmem] + [vmem] * len(others + gathered),
        out_specs=vmem,
        scratch_shapes=[
            VMEM((dp_count, row_count, tokens), BF16),
            VMEM((mp_count, PAD, edge), F32),
        ],
        compiler_params=pltpu.CompilerParams(vmem_limit_bytes=20 * 1024 * 1024),
    )(owner_of, slot_of, own, *others, *gathered)
    incoming = lax.all_to_all(outgoing, "mp", split_axis=0, concat_axis=0, tiled=True)

    count = REFRESH_MOST * 2
    factors_next, roots_next, homeward = pl.pallas_call(
        owner_kernel,
        out_shape=(
            jax.ShapeDtypeStruct(factors.shape[1:], F32),
            jax.ShapeDtypeStruct(roots.shape[1:], BF16),
            jax.ShapeDtypeStruct((mp_count, edge + PAD, edge), jnp.int16),
        ),
        in_specs=[smem, smem, smem, vmem, vmem, vmem],
        out_specs=(hbm, hbm, vmem),
        scratch_shapes=[
            VMEM(factors.shape[1:], F32),
            VMEM(roots.shape[1:], BF16),
            VMEM((mp_count, PAD, edge), F32),
            VMEM((slots, 2, edge, edge), BF16),
            VMEM((slots, edge + PAD, edge), jnp.int16),
            VMEM((count, edge, edge), F32),
            VMEM((count, edge, edge), F32),
            SMEM((slots + 1,), jnp.int32),
            SMEM((REFRESH_MOST + 1,), jnp.int32),
            pltpu.SemaphoreType.DMA((slots,)),
            pltpu.SemaphoreType.DMA,
        ],
        compiler_params=pltpu.CompilerParams(vmem_limit_bytes=28 * 1024 * 1024),
    )(owner_of, slot_of, refresh_ids, incoming, factors[0], roots[0])
    returned = lax.all_to_all(homeward, "mp", split_axis=0, concat_axis=0, tiled=True)

    local_blocks = owner_of.shape[1]
    direction = pl.pallas_call(
        functools.partial(home_kernel, edge),
        out_shape=jax.ShapeDtypeStruct((row_count, slab), F32),
        in_specs=[smem, vmem],
        out_specs=hbm,
        scratch_shapes=[
            VMEM((local_blocks, edge, edge), F32),
            pltpu.SemaphoreType.DMA((local_blocks,)),
        ],
    )(owner_of, returned)
    return (direction, factors_next[None], roots_next[None])


def solution(mesh):
    in_specs = (
        P("dp", None),
        P("dp", "mp"),
        P("dp", "mp", None, None, None),
        P("dp", "mp", None, None, None),
        P(),
        P(),
        P(),
    )
    out_specs = (P("dp", "mp"), P("dp", "mp", None, None, None), P("dp", "mp", None, None, None))
    return jax.shard_map(body, mesh=mesh, in_specs=in_specs, out_specs=out_specs, check_vma=False)
```
